32 devices in a mesh: dp: 4 (over z), row: 2 (over y), col: 4 (over x, core).
Axes of the slice: x: 2, y: 2, z: 4, core: 2. Of those that a mesh axis runs over, the one named last changes fastest.
Arguments:
- hidden: bfloat16 [1024, 14336], P(('dp', 'col'), 'row'), may hold values from -6 to 6
- weight_blocks: bfloat16 [2, 4, 320, 128, 128], P('row', 'col'), may hold values from -0.0625 to 0.0625
- kept_blocks: int32 [2, 4, 320], P('row', 'col'), may hold values from -1 to 447, as said below
- cotangent: bfloat16 [1024, 4096], P(('dp', 'row'), 'col'), may hold values from -6 to 6
Outputs:
- output: bfloat16 [1024, 4096], P(('dp', 'row'), 'col')
- input_grad: bfloat16 [1024, 14336], P(('dp', 'col'), 'row')
- weight_grad: bfloat16 [2, 4, 320, 128, 128], P('row', 'col', 'dp')
The draws below stay inside these ranges and needn't reach their ends.
Inputs may be any that keep to these rules, and one draw needn't show every extreme that they name: `kept_blocks`: entry s of grid position (i, j) names a block of that position's region by its local index, local block row times C plus local block column, with C = 8; entries of one position are distinct; -1 marks an empty slot, and empty slots come after the used ones. Each position uses between R C - 320 and 320 slots, with R = 56; some position uses all 320.
All inputs are finite; a program needn't handle non-finite values.
Results may differ from the reference program's by a relative error of at most 0.009.
Values may be sent and summed in bfloat16 or wider, within the bound.
No kernel may reach another device: no remote copies, remote signals or barrier semaphores. Data moves between devices by JAX's collectives and lax.ppermute only.
A program may use at most 192 MiB of HBM per device.

```python
import jax
import jax.numpy as jnp
from jax import lax

D = 4096
FF = 14336
BLOCK = 128
TOK = 256
TOKENS = 1024
CAP = 320
N_DP = 4
N_ROW = 2
N_COL = 4


def draw_kept_blocks(key, part):
    key = jax.random.fold_in(key, 11)
    region = FF // (BLOCK * N_ROW) * (D // (BLOCK * N_COL))
    devices_here = N_ROW * N_COL
    fewest = region - CAP
    count_seed, full_seed, order_seed = jax.random.split(key, 3)
    counts = jax.random.randint(count_seed, (devices_here,), fewest, CAP + 1)
    fullest = jax.random.randint(full_seed, (), 0, devices_here)
    counts = jnp.where(jnp.arange(devices_here) == fullest, CAP, counts)
    order_seeds = jax.random.split(order_seed, devices_here)
    orders = jax.vmap(lambda one_seed: jax.random.permutation(one_seed, region))(order_seeds)[:, :CAP]
    places = jnp.arange(CAP)[None, :]
    chosen = jnp.where(places < counts[:, None], orders, -1)
    return chosen.reshape(N_ROW, N_COL, CAP).astype(jnp.int32)


def level_of(own_key, shape, shards, least, top_value):
    def one(position, shards_of):
        steps = jax.random.uniform(jax.random.fold_in(jax.random.fold_in(own_key, 6), position), (shards_of,), jnp.float32, least / len(shards), top_value / len(shards))
        return jnp.repeat(jnp.exp(steps), shape[position] // shards_of).reshape((-1,) + (1,) * (len(shape) - position - 1))

    factor_of = one(*shards[0])
    for cut in shards[1:]:
        factor_of = factor_of * one(*cut)
    return factor_of


def scatter_about(rng, dims, scale, most, cuts=(), kind=jnp.bfloat16):
    array = jax.random.normal(rng, dims, jnp.float32) * scale
    if len(cuts) > 0:
        array = level_of(rng, dims, cuts, -0.22, 0.18) * array
    return jnp.clip(array, min=-most, max=most).astype(kind)


def setup_inputs(seed: int = 0) -> dict:
    splits = jax.random.split(jax.random.key(seed), 5)
    hidden = scatter_about(splits[0], (TOKENS, FF), 1.0, 6.0, ((0, 16), (1, 2)))
    weight_blocks = scatter_about(splits[1], (N_ROW, N_COL, CAP, BLOCK, BLOCK), (FF // 2) ** -0.5, 0.0625, ((0, 2), (1, 4)))
    kept_blocks = draw_kept_blocks(jax.random.fold_in(splits[4], 71), 0)
    cotangent = scatter_about(splits[3], (TOKENS, D), 1.0, 6.0, ((0, 8), (1, 4)))
    return {"hidden": hidden, "weight_blocks": weight_blocks, "kept_blocks": kept_blocks, "cotangent": cotangent}


def build_dense(weight_blocks, kept_blocks):
    reach_rows = FF // (BLOCK * N_ROW)
    reach_cols = D // (BLOCK * N_COL)
    usable = kept_blocks >= 0
    clamped = jnp.where(usable, kept_blocks, 0).astype(jnp.int32)
    grid_rows = jnp.arange(N_ROW, dtype=jnp.int32)[:, None, None] * reach_rows + clamped // reach_cols
    grid_cols = jnp.arange(N_COL, dtype=jnp.int32)[None, :, None] * reach_cols + clamped % reach_cols
    values = weight_blocks.astype(jnp.float32) * usable[..., None, None].astype(jnp.float32)
    dense_blocks = jnp.zeros((FF // BLOCK, D // BLOCK, BLOCK, BLOCK), jnp.float32)
    dense_blocks = dense_blocks.at[grid_rows, grid_cols].add(values)
    return dense_blocks.transpose(0, 2, 1, 3).reshape(FF, D), grid_rows, grid_cols, usable


def rounded(value):
    return lax.optimization_barrier(value.astype(jnp.bfloat16)).astype(jnp.float32)


def reference(hidden, weight_blocks, kept_blocks, cotangent):
    dense_weight, grid_rows, grid_cols, usable = build_dense(weight_blocks, kept_blocks)
    hidden_wide = hidden.astype(jnp.float32)
    grad_wide = cotangent.astype(jnp.float32)
    share_rows = FF // N_ROW
    share_cols = D // N_COL
    output = jnp.zeros((TOKENS, D), jnp.float32)
    for index in range(N_ROW):
        lower = index * share_rows
        piece = jnp.dot(hidden_wide[:, lower:lower + share_rows], dense_weight[lower:lower + share_rows],
                        precision=lax.Precision.HIGHEST)
        output = output + rounded(piece)
    input_grad = jnp.zeros((TOKENS, FF), jnp.float32)
    for index in range(N_COL):
        lower = index * share_cols
        piece = jnp.dot(grad_wide[:, lower:lower + share_cols], dense_weight[:, lower:lower + share_cols].T,
                        precision=lax.Precision.HIGHEST)
        input_grad = input_grad + rounded(piece)
    dense_grad = jnp.zeros((FF, D), jnp.float32)
    for replica in range(N_DP):
        lower = replica * TOK
        piece = jnp.dot(hidden_wide[lower:lower + TOK].T, grad_wide[lower:lower + TOK],
                        precision=lax.Precision.HIGHEST) / TOK
        dense_grad = dense_grad + rounded(piece)
    picked = dense_grad.reshape(FF // BLOCK, BLOCK, D // BLOCK, BLOCK)[grid_rows, :, grid_cols, :]
    weight_grad = picked * usable[..., None, None].astype(jnp.float32)
    return output.astype(jnp.bfloat16), input_grad.astype(jnp.bfloat16), weight_grad.astype(jnp.bfloat16)
```

```python
import functools

import jax
import jax.numpy as jnp
from jax import lax
from jax.experimental import pallas as pl
from jax.experimental.pallas import tpu as pltpu
from jax.sharding import PartitionSpec as P

VMEM = pltpu.VMEM
SMEM = pltpu.SMEM
LIMIT = 56 * 1024 * 1024


def whole(space):
    return pl.BlockSpec(memory_space=space)


def tile_of(size, most):
    best = 128
    for tile in range(128, most + 1, 128):
        if size % tile == 0:
            best = tile
    return best


def build_kernel(kept, blocks, dense):
    slots, block, _ = blocks.shape
    rows, cols = dense.shape
    col_blocks = cols // block

    def clear(index, carry):
        dense[pl.ds(pl.multiple_of(index * block, block), block), :] = jnp.zeros((block, cols), dense.dtype)
        return carry

    lax.fori_loop(0, rows // block, clear, 0)

    def place(slot, carry):
        chosen = kept[slot]

        @pl.when(chosen >= 0)
        def _():
            top = pl.multiple_of((chosen // col_blocks) * block, block)
            left = pl.multiple_of((chosen % col_blocks) * block, block)
            dense[pl.ds(top, block), pl.ds(left, block)] = blocks[slot]

        return carry

    lax.fori_loop(0, slots, place, 0)


def build_dense(kept, blocks, rows, cols):
    return pl.pallas_call(
        build_kernel,
        out_shape=jax.ShapeDtypeStruct((rows, cols), blocks.dtype),
        in_specs=[whole(SMEM), whole(VMEM)],
        out_specs=whole(VMEM),
        compiler_params=pltpu.CompilerParams(vmem_limit_bytes=LIMIT),
        cost_estimate=pl.CostEstimate(flops=0, bytes_accessed=2 * (blocks.size + rows * cols), transcendentals=0),
        name="build_dense",
    )(kept, blocks)


def input_kernel(grad, dense, keep, send):
    half = keep.shape[0]
    part = lax.dot_general(grad[...], dense[...], (((1,), (1,)), ((), ())), preferred_element_type=jnp.float32)
    keep[...] = part[:half].astype(keep.dtype)
    send[...] = part[half:].astype(send.dtype)


def input_partial(grad, dense):
    tokens, cols = grad.shape
    rows = dense.shape[0]
    tile = tile_of(rows, 512)
    shape = jax.ShapeDtypeStruct((tokens // 2, rows), grad.dtype)
    spec = pl.BlockSpec((tokens // 2, tile), lambda t: (0, t))
    return pl.pallas_call(
        input_kernel,
        grid=(rows // tile,),
        out_shape=(shape, shape),
        in_specs=[pl.BlockSpec((tokens, cols), lambda t: (0, 0)), pl.BlockSpec((tile, cols), lambda t: (t, 0))],
        out_specs=(spec, spec),
        compiler_params=pltpu.CompilerParams(vmem_limit_bytes=LIMIT),
        cost_estimate=pl.CostEstimate(
            flops=2 * tokens * rows * cols, bytes_accessed=2 * (rows * cols + tokens * (rows + cols)), transcendentals=0
        ),
        name="input_partial",
    )(grad, dense)


def output_kernel(count, order, *refs):
    pieces, dense, out, total = refs[:count], refs[count], refs[count + 1], refs[count + 2]
    step = pl.program_id(0)
    group = pieces[0].shape[0]
    hidden = jnp.concatenate([piece[...] for piece in pieces], axis=0)
    part = jnp.dot(hidden, dense[...], preferred_element_type=jnp.float32)

    @pl.when(step == 0)
    def _():
        total[...] = part

    @pl.when(step > 0)
    def _():
        total[...] += part

    @pl.when(step == pl.num_programs(0) - 1)
    def _():
        for index in range(count):
            start = pl.multiple_of(order[index] * group, group)
            out[pl.ds(start, group), :] = total[index * group:(index + 1) * group, :].astype(out.dtype)


def output_partial(order, pieces, dense):
    count = len(pieces)
    group, rows = pieces[0].shape
    tokens = group * count
    cols = dense.shape[1]
    tile = tile_of(rows, 512)
    return pl.pallas_call(
        functools.partial(output_kernel, count),
        grid=(rows // tile,),
        out_shape=jax.ShapeDtypeStruct((tokens, cols), pieces[0].dtype),
        in_specs=[whole(SMEM)]
        + [pl.BlockSpec((group, tile), lambda t: (0, t))] * count
        + [pl.BlockSpec((tile, cols), lambda t: (t, 0))],
        out_specs=pl.BlockSpec((tokens, cols), lambda t: (0, 0)),
        scratch_shapes=[pltpu.VMEM((tokens, cols), jnp.float32)],
        compiler_params=pltpu.CompilerParams(vmem_limit_bytes=LIMIT),
        cost_estimate=pl.CostEstimate(
            flops=2 * tokens * rows * cols, bytes_accessed=2 * (rows * cols + tokens * (rows + cols)), transcendentals=0
        ),
        name="output_partial",
    )(order, *pieces, dense)


def weight_kernel(count, first, last, scale, kept, *refs):
    pieces, turned = refs[:count], refs[count]
    before = None if first else refs[count + 1]
    out = refs[-1]
    slots, block, _ = out.shape
    col_blocks = turned.shape[0] // block

    def one(slot, carry):
        chosen = kept[slot]
        place = jnp.maximum(chosen, 0)
        top = pl.multiple_of((place // col_blocks) * block, block)
        left = pl.multiple_of((place % col_blocks) * block, block)
        hidden = jnp.concatenate([piece[:, pl.ds(top, block)] for piece in pieces], axis=0)
        part = jnp.dot(turned[pl.ds(left, block), :], hidden, preferred_element_type=jnp.float32)
        if not first:
            part = part + before[slot]
        if last:
            part = jnp.where(chosen >= 0, part * scale, 0.0).T
        out[slot] = part.astype(out.dtype)
        return carry

    lax.fori_loop(0, slots, one, 0, unroll=4 if slots % 4 == 0 else 1)


def weight_partial(kept, pieces, turned, before, block, scale, last):
    count = len(pieces)
    slots = kept.shape[0]
    first = before is None
    tokens = turned.shape[1]
    extra = () if first else (before,)
    kind = jnp.bfloat16 if last else jnp.float32
    return pl.pallas_call(
        functools.partial(weight_kernel, count, first, last, scale),
        out_shape=jax.ShapeDtypeStruct((slots, block, block), kind),
        in_specs=[whole(SMEM)] + [whole(VMEM)] * (count + 1 + len(extra)),
        out_specs=whole(VMEM),
        compiler_params=pltpu.CompilerParams(vmem_limit_bytes=LIMIT),
        cost_estimate=pl.CostEstimate(
            flops=8 * slots * tokens * block * block,
            bytes_accessed=2 * tokens * pieces[0].shape[1] + 8 * slots * block * block,
            transcendentals=0,
        ),
        name="weight_partial",
    )(kept, *pieces, turned, *extra)


def on_device(n_dp, n_row, n_col, hidden, weight_blocks, kept_blocks, cotangent):
    block = weight_blocks.shape[-1]
    slots = weight_blocks.shape[2]
    blocks = weight_blocks.reshape(slots, block, block)
    kept = kept_blocks.reshape(slots)
    group, rows = hidden.shape
    part_rows, cols = cotangent.shape
    tokens = group * n_col
    n_hi = n_col // 2
    dp, row, col = lax.axis_index("dp"), lax.axis_index("row"), lax.axis_index("col")
    share = slots // n_dp
    own_kept = lax.dynamic_slice_in_dim(kept, dp * share, share)
    hi, core = col // 2, col % 2
    mine = [((hi + step) % n_hi) * 2 + core for step in range(n_hi)]
    other = [((hi + step) % n_hi) * 2 + 1 - core for step in range(n_hi)]
    order = jnp.stack(mine + other).astype(jnp.int32)

    def shift(value, axis, size, step):
        return lax.ppermute(value, axis, [(index, (index + step) % size) for index in range(size)])

    def over_x(value, step):
        return lax.ppermute(
            value, "col", [(((index // 2 + step) % n_hi) * 2 + index % 2, index) for index in range(n_col)]
        )

    def to_x(value, step):
        return lax.ppermute(
            value, "col", [(index, ((index // 2 + step) % n_hi) * 2 + index % 2) for index in range(n_col)]
        )

    def swap(value):
        return lax.ppermute(value, "col", [(index, index ^ 1) for index in range(n_col)])

    def spread(value):
        near = [value] + [over_x(value, step) for step in range(1, n_hi)]
        return near + [swap(piece) for piece in near]

    def all_rows(value):
        held = [value] + [shift(value, "row", n_row, step) for step in range(1, n_row)]
        stacked = jnp.stack(held)
        return jnp.take(stacked, (row - jnp.arange(n_row)) % n_row, axis=0).reshape(tokens, cols)

    def arranged(value):
        return jnp.take(value.reshape(n_col, group, cols), order, axis=0).reshape(tokens, cols)

    grads = [arranged(all_rows(cotangent if step == 0 else shift(cotangent, "dp", n_dp, step))) for step in range(n_dp)]
    dense = build_dense(kept, blocks, rows, cols)

    keep, send = input_partial(grads[0], dense)
    got = swap(send)
    pair = (keep.astype(jnp.float32) + got.astype(jnp.float32)).reshape(n_hi, group, rows)
    input_grad = pair[0]
    for step in range(1, n_hi):
        input_grad = input_grad + to_x(pair[step].astype(jnp.bfloat16), step).astype(jnp.float32)
    input_grad = input_grad.astype(jnp.bfloat16)

    own = spread(hidden)
    part = output_partial(order, own, dense).reshape(n_row, part_rows, cols)
    output = lax.dynamic_index_in_dim(part, row, 0, keepdims=False).astype(jnp.float32)
    for step in range(1, n_row):
        piece = lax.dynamic_index_in_dim(part, (row + step) % n_row, 0, keepdims=False)
        output = output + shift(piece, "row", n_row, step).astype(jnp.float32)
    output = output.astype(jnp.bfloat16)

    total = None
    visits = [0] + sorted(range(1, n_dp), key=lambda step: min(step, n_dp - step))
    for place, step in enumerate(visits):
        pieces = own if step == 0 else spread(shift(hidden, "dp", n_dp, step))
        total = weight_partial(
            own_kept, pieces, grads[step].T, total, block, 1.0 / tokens, place == n_dp - 1
        )
    return output, input_grad, total.reshape(1, 1, share, block, block)


def solution(mesh):
    in_specs = (
        P(("dp", "col"), "row"),
        P("row", "col", None, None, None),
        P("row", "col", None),
        P(("dp", "row"), "col"),
    )
    out_specs = (
        P(("dp", "row"), "col"),
        P(("dp", "col"), "row"),
        P("row", "col", "dp", None, None),
    )
    sizes = (mesh.shape["dp"], mesh.shape["row"], mesh.shape["col"])
    return jax.shard_map(
        functools.partial(on_device, *sizes), mesh=mesh, in_specs=in_specs, out_specs=out_specs, check_vma=False
    )
```

```python
import functools

import jax
import jax.numpy as jnp
from jax import lax
from jax.experimental import pallas as pl
from jax.experimental.pallas import tpu as pltpu
from jax.sharding import PartitionSpec as P

MIB = 1024 * 1024
COST = pl.CostEstimate(flops=1000, bytes_accessed=1000, transcendentals=0)


def whole(space):
    return pl.BlockSpec(memory_space=space)


def params(mib):
    return pltpu.CompilerParams(vmem_limit_bytes=mib * MIB)


def after(value, *others):
    return lax.optimization_barrier((value, *others))[0]


def tile_of(size, block, most):
    best = block
    for tile in range(block, most + 1, block):
        if size % tile == 0:
            best = tile
    return best


def group_order(n_col):
    col = lax.axis_index("col")
    hi, core, n_hi = col // 2, col % 2, n_col // 2
    near = [((hi + step) % n_hi) * 2 + core for step in range(n_hi)]
    return near + [index + 1 - 2 * core for index in near]


def in_order(parts, natural, n_row):
    row = lax.axis_index("row")
    for step, part in enumerate(parts):
        size = part.shape[0]
        start = pl.multiple_of(((row - step + n_row) % n_row) * size, size)
        natural[pl.ds(start, size), :] = part[...]


def input_kernel(n_row, n_col, slot_of, blocks, *refs):
    parts, refs = refs[:n_row], refs[n_row:]
    sums, (send, dense, natural, grad) = refs[:n_col // 2], refs[n_col // 2:]
    step = pl.program_id(0)
    tile, cols = dense.shape
    block = blocks.shape[1]
    col_blocks = cols // block
    group = sums[0].shape[0]

    @pl.when(step == 0)
    def _():
        in_order(parts, natural, n_row)
        for place, index in enumerate(group_order(n_col)):
            start = pl.multiple_of(index * group, group)
            grad[place * group:(place + 1) * group, :] = natural[pl.ds(start, group), :]

    first = step * (tile // block) * col_blocks

    def row_of_blocks(index, carry):
        top = pl.multiple_of(index * block, block)
        for side in range(col_blocks):
            slot = slot_of[first + index * col_blocks + side]
            values = blocks[jnp.maximum(slot, 0)]
            dense[pl.ds(top, block), side * block:(side + 1) * block] = jnp.where(slot >= 0, values, jnp.zeros_like(values))
        return carry

    lax.fori_loop(0, tile // block, row_of_blocks, 0)
    part = lax.dot_general(grad[...], dense[...], (((1,), (1,)), ((), ())), preferred_element_type=jnp.float32)
    for place, ref in enumerate(sums):
        ref[...] = part[place * group:(place + 1) * group].astype(ref.dtype)
    send[...] = part[n_col // 2 * group:].astype(send.dtype)


def input_partial(n_row, n_col, slot_of, blocks, parts, rows):
    part_rows, cols = parts[0].shape
    tokens = part_rows * n_row
    kind = blocks.dtype
    tile = tile_of(rows, blocks.shape[1], 1792)
    group, n_hi = tokens // n_col, n_col // 2
    shapes = [jax.ShapeDtypeStruct((height, rows), kind) for height in [group] * n_hi + [tokens // 2]]
    specs = [pl.BlockSpec((height, tile), lambda t: (0, t)) for height in [group] * n_hi + [tokens // 2]]
    return pl.pallas_call(
        functools.partial(input_kernel, n_row, n_col),
        grid=(rows // tile,),
        out_shape=(*shapes, jax.ShapeDtypeStruct((rows, cols), kind)),
        in_specs=[whole(pltpu.SMEM)] + [whole(pltpu.VMEM)] * (1 + n_row),
        out_specs=(*specs, pl.BlockSpec((tile, cols), lambda t: (t, 0))),
        scratch_shapes=[pltpu.VMEM((tokens, cols), kind), pltpu.VMEM((tokens, cols), kind)],
        compiler_params=params(44),
        cost_estimate=COST,
        name="input_partial",
    )(slot_of, blocks, *parts)


def output_kernel(n_col, *refs):
    pieces, (dense, out, total) = refs[:n_col], refs[n_col:]
    step = pl.program_id(0)
    group = pieces[0].shape[0]
    hidden = jnp.concatenate([piece[...] for piece in pieces], axis=0)
    part = jnp.dot(hidden, dense[...], preferred_element_type=jnp.float32)

    @pl.when(step == 0)
    def _():
        total[...] = part

    @pl.when(step > 0)
    def _():
        total[...] += part

    @pl.when(step == pl.num_programs(0) - 1)
    def _():
        for place, index in enumerate(group_order(n_col)):
            start = pl.multiple_of(index * group, group)
            out[pl.ds(start, group), :] = total[place * group:(place + 1) * group, :].astype(out.dtype)


def output_partial(n_col, pieces, dense):
    group, rows = pieces[0].shape
    tokens = group * n_col
    cols = dense.shape[1]
    tile = tile_of(rows, 128, 1792)
    return pl.pallas_call(
        functools.partial(output_kernel, n_col),
        grid=(rows // tile,),
        out_shape=jax.ShapeDtypeStruct((tokens, cols), pieces[0].dtype),
        in_specs=[pl.BlockSpec((group, tile), lambda t: (0, t))] * n_col + [pl.BlockSpec((tile, cols), lambda t: (t, 0))],
        out_specs=pl.BlockSpec((tokens, cols), lambda t: (0, 0)),
        scratch_shapes=[pltpu.VMEM((tokens, cols), jnp.float32)],
        compiler_params=params(20),
        cost_estimate=COST,
        name="output_partial",
    )(*pieces, dense)


def weight_kernel(n_dp, n_row, n_col, plan, first, last, scale, kept, *refs):
    count = sum(len(places) for _, places in plan)
    sets = sum(choices for choices, _ in plan) * n_row
    held, refs = refs[:sets], refs[sets:]
    pieces, refs = refs[:count], refs[count:]
    before, refs = (None, refs) if first else (refs[0], refs[1:])
    out, natural, turned = refs
    some_slots, block, _ = out.shape
    group = pieces[0].shape[0]
    col_blocks = turned.shape[0] // block
    order = group_order(n_col)
    dp = lax.axis_index("dp")
    step = pl.program_id(0)
    start_slot = (dp * pl.num_programs(0) + step) * some_slots

    @pl.when(step == 0)
    def _():
        offset, ref = 0, 0
        row = lax.axis_index("row")
        for choices, places in plan:
            for back in range(n_row):
                part = held[ref + back][...]
                if choices == 2:
                    part = jnp.where((dp == 0) | (dp == n_dp - 1), part, held[ref + n_row + back][...])
                size, strips = part.shape[0], part.shape[1] // natural.shape[1]
                for strip in range(strips):
                    start = (((row - back + n_row) % n_row) * strips + strip) * size
                    values = part[:, strip * natural.shape[1]:(strip + 1) * natural.shape[1]]
                    natural[pl.ds(pl.multiple_of(start, size), size), :] = values
            for place in places:
                rows = pl.ds(pl.multiple_of(order[place] * group, group), group)
                turned[:, offset:offset + group] = natural[rows, :].T
                offset += group
            ref += choices * n_row

    at_once = max(size for size in (1, 2, 4, 5, 8) if some_slots % size == 0)

    def some(turn, carry):
        results = []
        for index in range(at_once):
            slot = turn * at_once + index
            chosen = kept[start_slot + slot]
            place = jnp.maximum(chosen, 0)
            top = pl.multiple_of((place // col_blocks) * block, block)
            left = pl.multiple_of((place % col_blocks) * block, block)
            hidden = jnp.concatenate([piece[:, pl.ds(top, block)] for piece in pieces], axis=0)
            part = jnp.dot(turned[pl.ds(left, block), :], hidden, preferred_element_type=jnp.float32)
            if not first:
                part = part + before[slot]
            if last:
                part = jnp.where(chosen >= 0, part * scale, 0.0).T
            results.append(part.astype(out.dtype))
        for index in range(at_once):
            out[turn * at_once + index] = results[index]
        return carry

    lax.fori_loop(0, some_slots // at_once, some, 0)


def weight_partial(sizes, kept, work, before, share, block, cols, scale, last):
    n_dp, n_row, n_col = sizes
    first = before is None
    plan = [(len(entry[0]), entry[1]) for entry in work]
    held = [part for entry in work for parts in entry[0] for part in parts]
    pieces = [piece for entry in work for piece in entry[2]]
    tokens = pieces[0].shape[0] * len(pieces)
    some_slots = share // 5 if share % 5 == 0 else share
    spec = pl.BlockSpec((some_slots, block, block), lambda t: (t, 0, 0))
    extra = [] if first else [before]
    return pl.pallas_call(
        functools.partial(weight_kernel, n_dp, n_row, n_col, plan, first, last, scale),
        grid=(share // some_slots,),
        out_shape=jax.ShapeDtypeStruct((share, block, block), jnp.bfloat16 if last else jnp.float32),
        in_specs=[whole(pltpu.SMEM)] + [whole(pltpu.VMEM)] * (len(held) + len(pieces)) + [spec] * len(extra),
        out_specs=spec,
        scratch_shapes=[
            pltpu.VMEM((n_row * held[0].size // cols, cols), jnp.bfloat16),
            pltpu.VMEM((cols, tokens), jnp.bfloat16),
        ],
        compiler_params=params(20),
        cost_estimate=COST,
        name="weight_partial",
    )(kept, *held, *pieces, *extra)


def on_device(sizes, hidden, weight_blocks, kept_blocks, cotangent):
    n_dp, n_row, n_col = sizes
    block = weight_blocks.shape[-1]
    slots = weight_blocks.shape[2]
    blocks = weight_blocks.reshape(slots, block, block)
    kept = kept_blocks.reshape(slots)
    group, rows = hidden.shape
    part_rows, cols = cotangent.shape
    tokens = group * n_col
    n_hi = n_col // 2
    share = slots // n_dp
    region = (rows // block) * (cols // block)
    dp, row = lax.axis_index("dp"), lax.axis_index("row")

    def shift(value, axis, size, step):
        return lax.ppermute(value, axis, [(index, (index + step) % size) for index in range(size)])

    def from_x(value, step):
        return lax.ppermute(
            value, "col", [(((index // 2 + step) % n_hi) * 2 + index % 2, index) for index in range(n_col)]
        )

    def to_x(value, step):
        return lax.ppermute(
            value, "col", [(index, ((index // 2 + step) % n_hi) * 2 + index % 2) for index in range(n_col)]
        )

    def swap(value):
        return lax.ppermute(value, "col", [(index, index ^ 1) for index in range(n_col)])

    def over_x(value):
        return [from_x(value, step) for step in range(1, n_hi)]

    def all_rows(value):
        return [value] + [shift(value, "row", n_row, step) for step in range(1, n_row)]

    def along(value, pairs):
        return lax.ppermute(value, "dp", pairs)

    every = list(range(n_col))
    call = functools.partial(weight_partial, sizes, kept, share=share, block=block, cols=cols, scale=1.0 / tokens)
    slot_of = jnp.max(
        jnp.where(
            kept[None, :] == jnp.arange(region, dtype=jnp.int32)[:, None], jnp.arange(slots, dtype=jnp.int32)[None, :], -1
        ),
        axis=1,
    )
    line = n_dp == 4 and n_hi == 2 and part_rows % group == 0
    near = [hidden] + over_x(hidden)
    own_parts = all_rows(cotangent)
    if line:
        ends, middle, outward = [(0, 1), (1, 0), (2, 3), (3, 2)], [(1, 2), (2, 1)], [(1, 0), (2, 3)]
        strips = range(0, part_rows, group)
        packed = jnp.concatenate([hidden] + [cotangent[start:start + group] for start in strips], axis=1)
        hop_a, hop_b = along(packed, ends), along(packed, middle)
    *sums, send, dense = input_partial(n_row, n_col, slot_of, blocks, own_parts, rows)

    got = swap(send)
    if line:
        hop_a, hop_b = after(hop_a, send), after(hop_b, send)
        hop_c, hop_d = along(hop_b, outward), along(hop_a, middle)
        swapped = [swap(after(hidden, send, hop_a, hop_b, *near[1:]))]
    else:
        swapped = [swap(hidden)]
    for value in near[1:]:
        swapped.append(swap(after(value, swapped[-1])))
    own = near + swapped
    got = after(got, *own)

    def pair(step):
        return sums[step].astype(jnp.float32) + got[step * group:(step + 1) * group].astype(jnp.float32)

    crossing = [pair(step).astype(jnp.bfloat16) for step in range(1, n_hi)]
    input_grad = pair(0)
    for step, value in enumerate(crossing):
        input_grad = input_grad + to_x(value, step + 1).astype(jnp.float32)
    input_grad = input_grad.astype(jnp.bfloat16)
    part = output_partial(n_col, own, after(dense, *crossing))

    parts = after(part, input_grad).reshape(n_row, part_rows, cols)
    output = lax.dynamic_index_in_dim(parts, row, 0, keepdims=False).astype(jnp.float32)
    for step in range(1, n_row):
        piece = lax.dynamic_index_in_dim(parts, (row + step) % n_row, 0, keepdims=False)
        output = output + shift(piece, "row", n_row, step).astype(jnp.float32)
    output = output.astype(jnp.bfloat16)
    total = call([([[after(own_parts[0], output)] + own_parts[1:]], every, own)], None, last=False)

    if line:
        inner = (dp == 1) | (dp == 2)

        def landed(own_hop, outer_hop):
            return [
                jnp.where(inner, own_hop[:, :rows], outer_hop[:, :rows]),
                jnp.where(inner, own_hop[:, rows:], outer_hop[:, rows:]),
            ]

        hop_c, hop_d = after(hop_c, part), after(hop_d, part)
        hop_e = along(hop_d, outward)
        second, grad_2 = landed(hop_b, hop_c)
        (far_2,) = over_x(after(second, input_grad))
        both = all_rows(after(jnp.concatenate([hop_a[:, rows:], grad_2], axis=0), input_grad))
        rows_1, rows_2 = [value[:group] for value in both], [value[group:] for value in both]

        hop_e = after(hop_e, total)
        third, grad_3 = landed(hop_d, hop_e)
        (far_3,) = over_x(after(third, far_2))
        far_1 = along(after(near[1], hop_e, far_2), ends)
        swap_1, swap_2 = swap(after(hop_a, far_2)), swap(after(second, far_2))
        rows_3 = all_rows(after(grad_3, far_2))
        swap_far_2, swap_3 = swap(after(far_2, swap_1, swap_2)), swap(after(third, swap_1, swap_2))
        work = [
            ([rows_1], [0, 2], [hop_a, swap_1]),
            ([rows_2], every, [second, far_2, swap_2, swap_far_2]),
            ([rows_3], [0, 2], [third, swap_3]),
        ]
        total = call(work, total, last=False)

        far_1, far_3 = after(far_1, total), after(far_3, total)
        work = [([rows_1], [1, 3], [far_1, swap(far_1)]), ([rows_3], [1, 3], [far_3, swap(far_3)])]
        total = call(work, total, last=True)
    else:
        for step in range(1, n_dp):
            piece = shift(hidden, "dp", n_dp, step)
            near = [piece] + over_x(piece)
            held = [all_rows(shift(cotangent, "dp", n_dp, step))]
            total = call([(held, every, near + [swap(value) for value in near])], total, last=step == n_dp - 1)
    return output, input_grad, total.reshape(1, 1, share, block, block)


def solution(mesh):
    in_specs = (
        P(("dp", "col"), "row"),
        P("row", "col", None, None, None),
        P("row", "col", None),
        P(("dp", "row"), "col"),
    )
    out_specs = (
        P(("dp", "row"), "col"),
        P(("dp", "col"), "row"),
        P("row", "col", "dp", None, None),
    )
    sizes = (mesh.shape["dp"], mesh.shape["row"], mesh.shape["col"])
    return jax.shard_map(
        functools.partial(on_device, sizes), mesh=mesh, in_specs=in_specs, out_specs=out_specs, check_vma=False
    )
```

```python
import functools

import jax
import jax.numpy as jnp
from jax import lax
from jax.experimental import pallas as pl
from jax.experimental.pallas import tpu as pltpu
from jax.sharding import PartitionSpec as P

MIB = 1024 * 1024
COST = pl.CostEstimate(flops=1000, bytes_accessed=1000, transcendentals=0)


def whole(space):
    return pl.BlockSpec(memory_space=space)


def params(mib):
    return pltpu.CompilerParams(vmem_limit_bytes=mib * MIB)


def after(value, *others):
    return lax.optimization_barrier((value, *others))[0]


def tile_of(size, block, most):
    best = block
    for tile in range(block, most + 1, block):
        if size % tile == 0:
            best = tile
    return best


def group_order(n_col):
    col = lax.axis_index("col")
    hi, core, n_hi = col // 2, col % 2, n_col // 2
    near = [((hi + step) % n_hi) * 2 + core for step in range(n_hi)]
    return near + [index + 1 - 2 * core for index in near]


def in_order(parts, natural, n_row):
    row = lax.axis_index("row")
    for step, part in enumerate(parts):
        size = part.shape[0]
        start = pl.multiple_of(((row - step + n_row) % n_row) * size, size)
        natural[pl.ds(start, size), :] = part[...]


def input_kernel(n_row, n_col, slot_of, blocks, *refs):
    parts, refs = refs[:n_row], refs[n_row:]
    sums, (dense, natural, grad) = refs[:n_col], refs[n_col:]
    step = pl.program_id(0)
    tile, cols = dense.shape
    block = blocks.shape[1]
    col_blocks = cols // block
    group = sums[0].shape[0]

    @pl.when(step == 0)
    def _():
        in_order(parts, natural, n_row)
        for place, index in enumerate(group_order(n_col)):
            start = pl.multiple_of(index * group, group)
            grad[place * group:(place + 1) * group, :] = natural[pl.ds(start, group), :]

    first = step * (tile // block) * col_blocks

    def row_of_blocks(index, carry):
        top = pl.multiple_of(index * block, block)
        for side in range(col_blocks):
            slot = slot_of[first + index * col_blocks + side]
            values = blocks[jnp.maximum(slot, 0)]
            dense[pl.ds(top, block), side * block:(side + 1) * block] = jnp.where(slot >= 0, values, jnp.zeros_like(values))
        return carry

    lax.fori_loop(0, tile // block, row_of_blocks, 0)
    part = lax.dot_general(grad[...], dense[...], (((1,), (1,)), ((), ())), preferred_element_type=jnp.float32)
    for place, ref in enumerate(sums):
        ref[...] = part[place * group:(place + 1) * group].astype(ref.dtype)


def input_partial(n_row, n_col, slot_of, blocks, parts, rows):
    part_rows, cols = parts[0].shape
    tokens = part_rows * n_row
    kind = blocks.dtype
    tile = tile_of(rows, blocks.shape[1], 1792)
    shapes = [jax.ShapeDtypeStruct((tokens // n_col, rows), kind)] * n_col
    specs = [pl.BlockSpec((tokens // n_col, tile), lambda t: (0, t))] * n_col
    return pl.pallas_call(
        functools.partial(input_kernel, n_row, n_col),
        grid=(rows // tile,),
        out_shape=(*shapes, jax.ShapeDtypeStruct((rows, cols), kind)),
        in_specs=[whole(pltpu.SMEM)] + [whole(pltpu.VMEM)] * (1 + n_row),
        out_specs=(*specs, pl.BlockSpec((tile, cols), lambda t: (t, 0))),
        scratch_shapes=[pltpu.VMEM((tokens, cols), kind), pltpu.VMEM((tokens, cols), kind)],
        compiler_params=params(44),
        cost_estimate=pl.CostEstimate(flops=16 * tokens * rows * cols, bytes_accessed=8 * rows * cols, transcendentals=0),
        name="input_partial",
    )(slot_of, blocks, *parts)


def pack_kernel(hidden, grad, out):
    group, rows = hidden.shape
    cols = grad.shape[1]
    out[:, :rows] = hidden[...]
    for strip in range(grad.shape[0] // group):
        out[:, rows + strip * cols:rows + (strip + 1) * cols] = grad[strip * group:(strip + 1) * group, :]


def pack(hidden, grad):
    group, rows = hidden.shape
    return pl.pallas_call(
        pack_kernel,
        out_shape=jax.ShapeDtypeStruct((group, rows + grad.size // group), hidden.dtype),
        in_specs=[whole(pltpu.VMEM)] * 2,
        out_specs=whole(pltpu.VMEM),
        compiler_params=params(8),
        cost_estimate=COST,
        name="pack",
    )(hidden, grad)


def pair_kernel(one, two, out):
    out[...] = (one[...].astype(jnp.float32) + two[...].astype(jnp.float32)).astype(out.dtype)


def pair_sum(one, two):
    height, rows = one.shape
    tile = tile_of(rows, 128, 3584)
    spec = pl.BlockSpec((height, tile), lambda t: (0, t))
    return pl.pallas_call(
        pair_kernel,
        grid=(rows // tile,),
        out_shape=jax.ShapeDtypeStruct(one.shape, one.dtype),
        in_specs=[spec, spec],
        out_specs=spec,
        compiler_params=params(8),
        cost_estimate=COST,
        name="pair_sum",
    )(one, two)


def output_kernel(n_col, *refs):
    pieces, (dense, out, total) = refs[:n_col], refs[n_col:]
    step = pl.program_id(0)
    group = pieces[0].shape[0]
    hidden = jnp.concatenate([piece[...] for piece in pieces], axis=0)
    part = jnp.dot(hidden, dense[...], preferred_element_type=jnp.float32)

    @pl.when(step == 0)
    def _():
        total[...] = part

    @pl.when(step > 0)
    def _():
        total[...] += part

    @pl.when(step == pl.num_programs(0) - 1)
    def _():
        for place, index in enumerate(group_order(n_col)):
            start = pl.multiple_of(index * group, group)
            out[pl.ds(start, group), :] = total[place * group:(place + 1) * group, :].astype(out.dtype)


def output_partial(n_col, pieces, dense):
    group, rows = pieces[0].shape
    tokens = group * n_col
    cols = dense.shape[1]
    tile = tile_of(rows, 128, 1792)
    return pl.pallas_call(
        functools.partial(output_kernel, n_col),
        grid=(rows // tile,),
        out_shape=jax.ShapeDtypeStruct((tokens, cols), pieces[0].dtype),
        in_specs=[pl.BlockSpec((group, tile), lambda t: (0, t))] * n_col + [pl.BlockSpec((tile, cols), lambda t: (t, 0))],
        out_specs=pl.BlockSpec((tokens, cols), lambda t: (0, 0)),
        scratch_shapes=[pltpu.VMEM((tokens, cols), jnp.float32)],
        compiler_params=params(20),
        cost_estimate=pl.CostEstimate(flops=16 * tokens * rows * cols, bytes_accessed=8 * rows * cols, transcendentals=0),
        name="output_partial",
    )(*pieces, dense)


def weight_kernel(n_dp, n_row, n_col, plan, first, last, scale, kept, *refs):
    count = sum(len(places) for _, places in plan)
    sets = sum(choices for choices, _ in plan) * n_row
    held, refs = refs[:sets], refs[sets:]
    pieces, refs = refs[:count], refs[count:]
    before, refs = (None, refs) if first else (refs[0], refs[1:])
    out, natural, turned = refs
    some_slots, block, _ = out.shape
    group = pieces[0].shape[0]
    col_blocks = turned.shape[0] // block
    order = group_order(n_col)
    dp = lax.axis_index("dp")
    step = pl.program_id(0)
    start_slot = (dp * pl.num_programs(0) + step) * some_slots

    @pl.when(step == 0)
    def _():
        offset, ref = 0, 0
        row = lax.axis_index("row")
        for choices, places in plan:
            for back in range(n_row):
                part = held[ref + back][...]
                if choices == 2:
                    part = jnp.where((dp == 0) | (dp == n_dp - 1), part, held[ref + n_row + back][...])
                size, strips = part.shape[0], part.shape[1] // natural.shape[1]
                for strip in range(strips):
                    start = (((row - back + n_row) % n_row) * strips + strip) * size
                    values = part[:, strip * natural.shape[1]:(strip + 1) * natural.shape[1]]
                    natural[pl.ds(pl.multiple_of(start, size), size), :] = values
            for place in places:
                rows = pl.ds(pl.multiple_of(order[place] * group, group), group)
                turned[:, offset:offset + group] = natural[rows, :].T
                offset += group
            ref += choices * n_row

    at_once = max(size for size in (1, 2, 4, 5, 8, 10, 20) if some_slots % size == 0)

    def some(turn, carry):
        results = []
        for index in range(at_once):
            slot = turn * at_once + index
            chosen = kept[start_slot + slot]
            place = jnp.maximum(chosen, 0)
            top = pl.multiple_of((place // col_blocks) * block, block)
            left = pl.multiple_of((place % col_blocks) * block, block)
            hidden = jnp.concatenate([piece[:, pl.ds(top, block)] for piece in pieces], axis=0)
            part = jnp.dot(turned[pl.ds(left, block), :], hidden, preferred_element_type=jnp.float32)
            if not first:
                part = part + before[slot]
            if last:
                part = jnp.where(chosen >= 0, part * scale, 0.0).T
            results.append(part.astype(out.dtype))
        for index in range(at_once):
            out[turn * at_once + index] = results[index]
        return carry

    lax.fori_loop(0, some_slots // at_once, some, 0)


def weight_partial(sizes, kept, work, before, share, block, cols, scale, last):
    n_dp, n_row, n_col = sizes
    first = before is None
    plan = [(len(entry[0]), entry[1]) for entry in work]
    held = [part for entry in work for parts in entry[0] for part in parts]
    pieces = [piece for entry in work for piece in entry[2]]
    tokens = pieces[0].shape[0] * len(pieces)
    some_slots = share // 4 if share % 4 == 0 else share
    spec = pl.BlockSpec((some_slots, block, block), lambda t: (t, 0, 0))
    extra = [] if first else [before]
    return pl.pallas_call(
        functools.partial(weight_kernel, n_dp, n_row, n_col, plan, first, last, scale),
        grid=(share // some_slots,),
        out_shape=jax.ShapeDtypeStruct((share, block, block), jnp.bfloat16 if last else jnp.float32),
        in_specs=[whole(pltpu.SMEM)] + [whole(pltpu.VMEM)] * (len(held) + len(pieces)) + [spec] * len(extra),
        out_specs=spec,
        scratch_shapes=[
            pltpu.VMEM((n_row * held[0].size // cols, cols), jnp.bfloat16),
            pltpu.VMEM((cols, tokens), jnp.bfloat16),
        ],
        compiler_params=params(20),
        cost_estimate=COST,
        name="weight_partial",
    )(kept, *held, *pieces, *extra)


def on_device(sizes, hidden, weight_blocks, kept_blocks, cotangent):
    n_dp, n_row, n_col = sizes
    block = weight_blocks.shape[-1]
    slots = weight_blocks.shape[2]
    blocks = weight_blocks.reshape(slots, block, block)
    kept = kept_blocks.reshape(slots)
    group, rows = hidden.shape
    part_rows, cols = cotangent.shape
    tokens = group * n_col
    n_hi = n_col // 2
    share = slots // n_dp
    region = (rows // block) * (cols // block)
    dp, row = lax.axis_index("dp"), lax.axis_index("row")

    def shift(value, axis, size, step):
        return lax.ppermute(value, axis, [(index, (index + step) % size) for index in range(size)])

    def from_x(value, step):
        return lax.ppermute(
            value, "col", [(((index // 2 + step) % n_hi) * 2 + index % 2, index) for index in range(n_col)]
        )

    def to_x(value, step):
        return lax.ppermute(
            value, "col", [(index, ((index // 2 + step) % n_hi) * 2 + index % 2) for index in range(n_col)]
        )

    def swap(value):
        return lax.ppermute(value, "col", [(index, index ^ 1) for index in range(n_col)])

    def over_x(value):
        return [from_x(value, step) for step in range(1, n_hi)]

    def all_rows(value):
        return [value] + [shift(value, "row", n_row, step) for step in range(1, n_row)]

    def along(value, pairs):
        return lax.ppermute(value, "dp", pairs)

    every = list(range(n_col))
    call = functools.partial(weight_partial, sizes, kept, share=share, block=block, cols=cols, scale=1.0 / tokens)
    slot_of = jnp.max(
        jnp.where(
            kept[None, :] == jnp.arange(region, dtype=jnp.int32)[:, None], jnp.arange(slots, dtype=jnp.int32)[None, :], -1
        ),
        axis=1,
    )
    line = n_dp == 4 and n_hi == 2 and part_rows % group == 0
    near = [hidden] + over_x(hidden)
    own_parts = all_rows(cotangent)
    if line:
        ends, middle, outward = [(0, 1), (1, 0), (2, 3), (3, 2)], [(1, 2), (2, 1)], [(1, 0), (2, 3)]
        packed = pack(hidden, cotangent)
        hop_a, hop_b = along(packed, ends), along(packed, middle)
    *sums, dense = input_partial(n_row, n_col, slot_of, blocks, own_parts, rows)

    crossing = [pair_sum(sums[step], after(swap(sums[n_hi + step]), *near[1:])) for step in range(1, n_hi)]
    if line:
        hop_a, hop_b = after(hop_a, *crossing), after(hop_b, *crossing)
        hop_c, hop_d = along(hop_b, outward), along(hop_a, middle)
        swapped = [swap(after(hidden, hop_a, hop_b))]
    else:
        swapped = [swap(hidden)]
    for value in near[1:]:
        swapped.append(swap(after(value, hop_a, hop_b) if line else value))
    own = near + swapped
    input_grad = sums[0].astype(jnp.float32) + after(swap(after(sums[n_hi], *crossing)), *own).astype(jnp.float32)
    for step, value in enumerate(crossing):
        input_grad = input_grad + to_x(value, step + 1).astype(jnp.float32)
    input_grad = input_grad.astype(jnp.bfloat16)
    part = output_partial(n_col, own, after(dense, *crossing))

    parts = after(part, input_grad).reshape(n_row, part_rows, cols)
    output = lax.dynamic_index_in_dim(parts, row, 0, keepdims=False).astype(jnp.float32)
    for step in range(1, n_row):
        piece = lax.dynamic_index_in_dim(parts, (row + step) % n_row, 0, keepdims=False)
        output = output + shift(piece, "row", n_row, step).astype(jnp.float32)
    output = output.astype(jnp.bfloat16)
    total = call([([[after(own_parts[0], output)] + own_parts[1:]], every, own)], None, last=False)

    if line:
        inner = (dp == 1) | (dp == 2)

        def landed(own_hop, outer_hop):
            return [
                jnp.where(inner, own_hop[:, :rows], outer_hop[:, :rows]),
                jnp.where(inner, own_hop[:, rows:], outer_hop[:, rows:]),
            ]

        hop_c, hop_d = after(hop_c, part), after(hop_d, part)
        hop_e = along(hop_d, outward)
        second, grad_2 = landed(hop_b, hop_c)
        (far_2,) = over_x(after(second, input_grad))
        both = all_rows(after(jnp.concatenate([hop_a[:, rows:], grad_2], axis=0), input_grad))
        rows_1, rows_2 = [value[:group] for value in both], [value[group:] for value in both]

        hop_e = after(hop_e, total)
        third, grad_3 = landed(hop_d, hop_e)
        (far_3,) = over_x(after(third, far_2))
        far_1 = along(after(near[1], hop_e, far_2), ends)
        swap_1, swap_2 = swap(after(hop_a, far_2)), swap(after(second, far_2))
        rows_3 = all_rows(after(grad_3, far_2))
        swap_far_2, swap_3 = swap(after(far_2, swap_1, swap_2)), swap(after(third, swap_1, swap_2))
        work = [
            ([rows_1], [0, 2], [hop_a, swap_1]),
            ([rows_2], every, [second, far_2, swap_2, swap_far_2]),
            ([rows_3], [0, 2], [third, swap_3]),
        ]
        total = call(work, total, last=False)

        far_1, far_3 = after(far_1, total), after(far_3, total)
        work = [([rows_1], [1, 3], [far_1, swap(far_1)]), ([rows_3], [1, 3], [far_3, swap(far_3)])]
        total = call(work, total, last=True)
    else:
        for step in range(1, n_dp):
            piece = shift(hidden, "dp", n_dp, step)
            near = [piece] + over_x(piece)
            held = [all_rows(shift(cotangent, "dp", n_dp, step))]
            total = call([(held, every, near + [swap(value) for value in near])], total, last=step == n_dp - 1)
    return output, input_grad, total.reshape(1, 1, share, block, block)


def solution(mesh):
    in_specs = (
        P(("dp", "col"), "row"),
        P("row", "col", None, None, None),
        P("row", "col", None),
        P(("dp", "row"), "col"),
    )
    out_specs = (
        P(("dp", "row"), "col"),
        P(("dp", "col"), "row"),
        P("row", "col", "dp", None, None),
    )
    sizes = (mesh.shape["dp"], mesh.shape["row"], mesh.shape["col"])
    return jax.shard_map(
        functools.partial(on_device, sizes), mesh=mesh, in_specs=in_specs, out_specs=out_specs, check_vma=False
    )
```

```python
import functools

import jax
import jax.numpy as jnp
from jax import lax
from jax.experimental import pallas as pl
from jax.experimental.pallas import tpu as pltpu
from jax.sharding import PartitionSpec as P

MIB = 1024 * 1024
COST = pl.CostEstimate(flops=1000, bytes_accessed=1000, transcendentals=0)


def whole(space):
    return pl.BlockSpec(memory_space=space)


def params(mib):
    return pltpu.CompilerParams(vmem_limit_bytes=mib * MIB)


def after(value, *others):
    return lax.optimization_barrier((value, *others))[0]


def tile_of(size, block, most):
    best = block
    for tile in range(block, most + 1, block):
        if size % tile == 0:
            best = tile
    return best


def group_order(n_col):
    col = lax.axis_index("col")
    hi, core, n_hi = col // 2, col % 2, n_col // 2
    near = [((hi + step) % n_hi) * 2 + core for step in range(n_hi)]
    return near + [index + 1 - 2 * core for index in near]


def in_order(parts, natural, n_row):
    row = lax.axis_index("row")
    for step, part in enumerate(parts):
        size = part.shape[0]
        start = pl.multiple_of(((row - step + n_row) % n_row) * size, size)
        natural[pl.ds(start, size), :] = part[...]


def input_kernel(n_row, n_col, slot_of, blocks, *refs):
    parts, refs = refs[:n_row], refs[n_row:]
    sums, (dense, natural, grad) = refs[:n_col], refs[n_col:]
    step = pl.program_id(0)
    tile, cols = dense.shape
    block = blocks.shape[1]
    col_blocks = cols // block
    group = sums[0].shape[0]

    @pl.when(step == 0)
    def _():
        in_order(parts, natural, n_row)
        for place, index in enumerate(group_order(n_col)):
            start = pl.multiple_of(index * group, group)
            grad[place * group:(place + 1) * group, :] = natural[pl.ds(start, group), :]

    first = step * (tile // block) * col_blocks

    def row_of_blocks(index, carry):
        top = pl.multiple_of(index * block, block)
        for side in range(col_blocks):
            slot = slot_of[first + index * col_blocks + side]
            values = blocks[jnp.maximum(slot, 0)]
            dense[pl.ds(top, block), side * block:(side + 1) * block] = jnp.where(slot >= 0, values, jnp.zeros_like(values))
        return carry

    lax.fori_loop(0, tile // block, row_of_blocks, 0)
    part = lax.dot_general(grad[...], dense[...], (((1,), (1,)), ((), ())), preferred_element_type=jnp.float32)
    for place, ref in enumerate(sums):
        ref[...] = part[place * group:(place + 1) * group].astype(ref.dtype)


def input_partial(n_row, n_col, slot_of, blocks, parts, rows):
    part_rows, cols = parts[0].shape
    tokens = part_rows * n_row
    kind = blocks.dtype
    tile = tile_of(rows, blocks.shape[1], 1792)
    shapes = [jax.ShapeDtypeStruct((tokens // n_col, rows), kind)] * n_col
    specs = [pl.BlockSpec((tokens // n_col, tile), lambda t: (0, t))] * n_col
    return pl.pallas_call(
        functools.partial(input_kernel, n_row, n_col),
        grid=(rows // tile,),
        out_shape=(*shapes, jax.ShapeDtypeStruct((rows, cols), kind)),
        in_specs=[whole(pltpu.SMEM)] + [whole(pltpu.VMEM)] * (1 + n_row),
        out_specs=(*specs, pl.BlockSpec((tile, cols), lambda t: (t, 0))),
        scratch_shapes=[pltpu.VMEM((tokens, cols), kind), pltpu.VMEM((tokens, cols), kind)],
        compiler_params=params(44),
        cost_estimate=pl.CostEstimate(flops=16 * tokens * rows * cols, bytes_accessed=8 * rows * cols, transcendentals=0),
        name="input_partial",
    )(slot_of, blocks, *parts)


def pack_kernel(hidden, grad, out):
    group, rows = hidden.shape
    cols = grad.shape[1]
    out[:, :rows] = hidden[...]
    for strip in range(grad.shape[0] // group):
        out[:, rows + strip * cols:rows + (strip + 1) * cols] = grad[strip * group:(strip + 1) * group, :]


def pack(hidden, grad):
    group, rows = hidden.shape
    return pl.pallas_call(
        pack_kernel,
        out_shape=jax.ShapeDtypeStruct((group, rows + grad.size // group), hidden.dtype),
        in_specs=[whole(pltpu.VMEM)] * 2,
        out_specs=whole(pltpu.VMEM),
        compiler_params=params(8),
        cost_estimate=COST,
        name="pack",
    )(hidden, grad)


def pair_kernel(one, two, out):
    out[...] = (one[...].astype(jnp.float32) + two[...].astype(jnp.float32)).astype(out.dtype)


def pair_sum(one, two):
    height, rows = one.shape
    tile = tile_of(rows, 128, 3584)
    spec = pl.BlockSpec((height, tile), lambda t: (0, t))
    return pl.pallas_call(
        pair_kernel,
        grid=(rows // tile,),
        out_shape=jax.ShapeDtypeStruct(one.shape, one.dtype),
        in_specs=[spec, spec],
        out_specs=spec,
        compiler_params=params(8),
        cost_estimate=COST,
        name="pair_sum",
    )(one, two)


def output_kernel(n_col, *refs):
    pieces, (dense, out, total) = refs[:n_col], refs[n_col:]
    step = pl.program_id(0)
    group = pieces[0].shape[0]
    hidden = jnp.concatenate([piece[...] for piece in pieces], axis=0)
    part = jnp.dot(hidden, dense[...], preferred_element_type=jnp.float32)

    @pl.when(step == 0)
    def _():
        total[...] = part

    @pl.when(step > 0)
    def _():
        total[...] += part

    @pl.when(step == pl.num_programs(0) - 1)
    def _():
        for place, index in enumerate(group_order(n_col)):
            start = pl.multiple_of(index * group, group)
            out[pl.ds(start, group), :] = total[place * group:(place + 1) * group, :].astype(out.dtype)


def output_partial(n_col, pieces, dense):
    group, rows = pieces[0].shape
    tokens = group * n_col
    cols = dense.shape[1]
    tile = tile_of(rows, 128, 1792)
    return pl.pallas_call(
        functools.partial(output_kernel, n_col),
        grid=(rows // tile,),
        out_shape=jax.ShapeDtypeStruct((tokens, cols), pieces[0].dtype),
        in_specs=[pl.BlockSpec((group, tile), lambda t: (0, t))] * n_col + [pl.BlockSpec((tile, cols), lambda t: (t, 0))],
        out_specs=pl.BlockSpec((tokens, cols), lambda t: (0, 0)),
        scratch_shapes=[pltpu.VMEM((tokens, cols), jnp.float32)],
        compiler_params=params(20),
        cost_estimate=pl.CostEstimate(flops=16 * tokens * rows * cols, bytes_accessed=8 * rows * cols, transcendentals=0),
        name="output_partial",
    )(*pieces, dense)


def weight_kernel(n_dp, n_row, n_col, plan, first, last, scale, kept, *refs):
    count = sum(len(places) for _, places in plan)
    sets = sum(choices for choices, _ in plan) * n_row
    held, refs = refs[:sets], refs[sets:]
    pieces, refs = refs[:count], refs[count:]
    before, refs = (None, refs) if first else (refs[0], refs[1:])
    out, natural, turned = refs
    some_slots, block, _ = out.shape
    group = pieces[0].shape[0]
    col_blocks = turned.shape[0] // block
    order = group_order(n_col)
    dp = lax.axis_index("dp")
    step = pl.program_id(0)
    start_slot = (dp * pl.num_programs(0) + step) * some_slots

    @pl.when(step == 0)
    def _():
        offset, ref = 0, 0
        row = lax.axis_index("row")
        for choices, places in plan:
            for back in range(n_row):
                part = held[ref + back][...]
                if choices == 2:
                    part = jnp.where((dp == 0) | (dp == n_dp - 1), part, held[ref + n_row + back][...])
                size, strips = part.shape[0], part.shape[1] // natural.shape[1]
                for strip in range(strips):
                    start = (((row - back + n_row) % n_row) * strips + strip) * size
                    values = part[:, strip * natural.shape[1]:(strip + 1) * natural.shape[1]]
                    natural[pl.ds(pl.multiple_of(start, size), size), :] = values
            for place in places:
                rows = pl.ds(pl.multiple_of(order[place] * group, group), group)
                turned[:, offset:offset + group] = natural[rows, :].T
                offset += group
            ref += choices * n_row

    at_once = max(size for size in (1, 2, 4, 5, 8, 10, 20) if some_slots % size == 0)

    def some(turn, carry):
        results = []
        for index in range(at_once):
            slot = turn * at_once + index
            chosen = kept[start_slot + slot]
            place = jnp.maximum(chosen, 0)
            top = pl.multiple_of((place // col_blocks) * block, block)
            left = pl.multiple_of((place % col_blocks) * block, block)
            hidden = jnp.concatenate([piece[:, pl.ds(top, block)] for piece in pieces], axis=0)
            part = jnp.dot(turned[pl.ds(left, block), :], hidden, preferred_element_type=jnp.float32)
            if not first:
                part = part + before[slot]
            if last:
                part = jnp.where(chosen >= 0, part * scale, 0.0).T
            results.append(part.astype(out.dtype))
        for index in range(at_once):
            out[turn * at_once + index] = results[index]
        return carry

    lax.fori_loop(0, some_slots // at_once, some, 0)


def weight_partial(sizes, kept, work, before, share, block, cols, scale, last):
    n_dp, n_row, n_col = sizes
    first = before is None
    plan = [(len(entry[0]), entry[1]) for entry in work]
    held = [part for entry in work for parts in entry[0] for part in parts]
    pieces = [piece for entry in work for piece in entry[2]]
    tokens = pieces[0].shape[0] * len(pieces)
    some_slots = share // 4 if share % 4 == 0 else share
    spec = pl.BlockSpec((some_slots, block, block), lambda t: (t, 0, 0))
    extra = [] if first else [before]
    return pl.pallas_call(
        functools.partial(weight_kernel, n_dp, n_row, n_col, plan, first, last, scale),
        grid=(share // some_slots,),
        out_shape=jax.ShapeDtypeStruct((share, block, block), jnp.bfloat16 if last else jnp.float32),
        in_specs=[whole(pltpu.SMEM)] + [whole(pltpu.VMEM)] * (len(held) + len(pieces)) + [spec] * len(extra),
        out_specs=spec,
        scratch_shapes=[
            pltpu.VMEM((n_row * held[0].size // cols, cols), jnp.bfloat16),
            pltpu.VMEM((cols, tokens), jnp.bfloat16),
        ],
        compiler_params=params(20),
        cost_estimate=COST,
        name="weight_partial",
    )(kept, *held, *pieces, *extra)


def on_device(sizes, hidden, weight_blocks, kept_blocks, cotangent):
    n_dp, n_row, n_col = sizes
    block = weight_blocks.shape[-1]
    slots = weight_blocks.shape[2]
    blocks = weight_blocks.reshape(slots, block, block)
    kept = kept_blocks.reshape(slots)
    group, rows = hidden.shape
    part_rows, cols = cotangent.shape
    tokens = group * n_col
    n_hi = n_col // 2
    share = slots // n_dp
    region = (rows // block) * (cols // block)
    dp, row = lax.axis_index("dp"), lax.axis_index("row")

    def shift(value, axis, size, step):
        return lax.ppermute(value, axis, [(index, (index + step) % size) for index in range(size)])

    def from_x(value, step):
        return lax.ppermute(
            value, "col", [(((index // 2 + step) % n_hi) * 2 + index % 2, index) for index in range(n_col)]
        )

    def to_x(value, step):
        return lax.ppermute(
            value, "col", [(index, ((index // 2 + step) % n_hi) * 2 + index % 2) for index in range(n_col)]
        )

    def swap(value):
        return lax.ppermute(value, "col", [(index, index ^ 1) for index in range(n_col)])

    def over_x(value):
        return [from_x(value, step) for step in range(1, n_hi)]

    def all_rows(value):
        return [value] + [shift(value, "row", n_row, step) for step in range(1, n_row)]

    def along(value, pairs):
        return lax.ppermute(value, "dp", pairs)

    every = list(range(n_col))
    call = functools.partial(weight_partial, sizes, kept, share=share, block=block, cols=cols, scale=1.0 / tokens)
    slot_of = jnp.max(
        jnp.where(
            kept[None, :] == jnp.arange(region, dtype=jnp.int32)[:, None], jnp.arange(slots, dtype=jnp.int32)[None, :], -1
        ),
        axis=1,
    )
    line = n_dp == 4 and n_hi == 2 and part_rows % group == 0
    packed = pack(hidden, cotangent) if line else hidden
    near = [hidden] + over_x(after(hidden, packed))
    own_parts = all_rows(cotangent)
    if line:
        ends, middle, outward = [(0, 1), (1, 0), (2, 3), (3, 2)], [(1, 2), (2, 1)], [(1, 0), (2, 3)]
        hop_a, hop_b = along(packed, ends), along(packed, middle)
    *sums, dense = input_partial(n_row, n_col, slot_of, blocks, own_parts, rows)

    crossing = [pair_sum(sums[step], after(swap(sums[n_hi + step]), *near[1:])) for step in range(1, n_hi)]
    if line:
        hop_a, hop_b = after(hop_a, *crossing), after(hop_b, *crossing)
        hop_c, hop_d = along(hop_b, outward), along(hop_a, middle)
        swapped = [swap(after(hidden, hop_a, hop_b))]
    else:
        swapped = [swap(hidden)]
    for value in near[1:]:
        swapped.append(swap(after(value, hop_a, hop_b) if line else value))
    own = near + swapped
    input_grad = sums[0].astype(jnp.float32) + after(swap(after(sums[n_hi], *crossing)), *own).astype(jnp.float32)
    for step, value in enumerate(crossing):
        input_grad = input_grad + to_x(value, step + 1).astype(jnp.float32)
    input_grad = input_grad.astype(jnp.bfloat16)
    part = output_partial(n_col, own, after(dense, *crossing))

    parts = after(part, input_grad).reshape(n_row, part_rows, cols)
    output = lax.dynamic_index_in_dim(parts, row, 0, keepdims=False).astype(jnp.float32)
    for step in range(1, n_row):
        piece = lax.dynamic_index_in_dim(parts, (row + step) % n_row, 0, keepdims=False)
        output = output + shift(piece, "row", n_row, step).astype(jnp.float32)
    output = output.astype(jnp.bfloat16)
    total = call([([[after(own_parts[0], output)] + own_parts[1:]], every, own)], None, last=False)

    if line:
        inner = (dp == 1) | (dp == 2)

        def landed(own_hop, outer_hop):
            return [
                jnp.where(inner, own_hop[:, :rows], outer_hop[:, :rows]),
                jnp.where(inner, own_hop[:, rows:], outer_hop[:, rows:]),
            ]

        hop_c, hop_d = after(hop_c, part), after(hop_d, part)
        hop_e = along(hop_d, outward)
        second, grad_2 = landed(hop_b, hop_c)
        (far_2,) = over_x(after(second, input_grad))
        both = all_rows(after(jnp.concatenate([hop_a[:, rows:], grad_2], axis=0), input_grad))
        rows_1, rows_2 = [value[:group] for value in both], [value[group:] for value in both]

        hop_e = after(hop_e, total)
        third, grad_3 = landed(hop_d, hop_e)
        (far_3,) = over_x(after(third, far_2))
        far_1 = along(after(near[1], hop_e, far_2), ends)
        swap_1, swap_2 = swap(after(hop_a, far_2)), swap(after(second, far_2))
        rows_3 = all_rows(after(grad_3, far_2))
        swap_far_2, swap_3 = swap(after(far_2, swap_1, swap_2)), swap(after(third, swap_1, swap_2))
        work = [
            ([rows_1], [0, 2], [hop_a, swap_1]),
            ([rows_2], every, [second, far_2, swap_2, swap_far_2]),
            ([rows_3], [0, 2], [third, swap_3]),
        ]
        total = call(work, total, last=False)

        far_1, far_3 = after(far_1, total), after(far_3, total)
        work = [([rows_1], [1, 3], [far_1, swap(far_1)]), ([rows_3], [1, 3], [far_3, swap(far_3)])]
        total = call(work, total, last=True)
    else:
        for step in range(1, n_dp):
            piece = shift(hidden, "dp", n_dp, step)
            near = [piece] + over_x(piece)
            held = [all_rows(shift(cotangent, "dp", n_dp, step))]
            total = call([(held, every, near + [swap(value) for value in near])], total, last=step == n_dp - 1)
    return output, input_grad, total.reshape(1, 1, share, block, block)


def solution(mesh):
    in_specs = (
        P(("dp", "col"), "row"),
        P("row", "col", None, None, None),
        P("row", "col", None),
        P(("dp", "row"), "col"),
    )
    out_specs = (
        P(("dp", "row"), "col"),
        P(("dp", "col"), "row"),
        P("row", "col", "dp", None, None),
    )
    sizes = (mesh.shape["dp"], mesh.shape["row"], mesh.shape["col"])
    return jax.shard_map(
        functools.partial(on_device, sizes), mesh=mesh, in_specs=in_specs, out_specs=out_specs, check_vma=False
    )
```
